32 devices in a mesh: groups: 1, expert: 16 (over z, y, core), dp: 2 (over x).
Axes of the slice: x: 2, y: 2, z: 4, core: 2. Of those that a mesh axis runs over, the one named last changes fastest.
Arguments:
- tokens: bfloat16 [768, 2048], P(('groups', 'expert', 'dp')), may hold values from -6 to 6
- targets: bfloat16 [768, 2048], P(('groups', 'expert', 'dp')), may hold values from -6 to 6
- expert_ids: int32 [768, 8], P(('groups', 'expert', 'dp')), may hold values from 0 to 15, all different within a row; in each aligned block of 24 rows (0 to 23, 24 to 47, ...) at most 13 rows name the same one
- gate_codes: int32 [768, 8], P(('groups', 'expert', 'dp')), may hold values from 1 to 255
- projections: bfloat16 [16, 2, 2048, 768], P('expert', None, None, 'dp'), may hold values from -0.125 to 0.125
- down_weight: bfloat16 [16, 768, 2048], P('expert', 'dp'), may hold values from -0.21875 to 0.21875
- direction: bfloat16 [16, 2048, 768], P('expert', None, 'dp'), may hold values from -0.125 to 0.125
Outputs:
- hvp: bfloat16 [16, 2048, 768], P(('groups', 'expert'), None, 'dp')
The draws below stay inside these ranges and needn't reach their ends.
Inputs may be any that keep to these rules, and one draw needn't show every extreme that they name: `expert_ids`: each row names 8 different experts. In each aligned block of 24 rows (the tokens of one device) no expert is named by more than 13 rows, and in some block one expert is named by exactly 13.
All inputs are finite; a program needn't handle non-finite values.
Results may differ from the reference program's by a relative error of at most 0.01.
Values may be sent and summed in bfloat16 or wider, within the bound.
A program may use at most 64 MiB of HBM per device.

```python
import math
from functools import partial
import jax
import jax.numpy as jnp
import numpy as np
from jax import lax

D = 2048
FF = 768
TOP = 8
EXP_DEV = 1
TOK_DEV = 24
EXPERTS = 16
MOST = 13
TOKENS = 768
N_EXPERT = 16
N_DP = 2


def touch_ends(values, own_key, smallest, top_value):
    longest = values.shape.index(max(values.shape))
    spots = []
    for shift in (0, 1):
        where = [jax.random.randint(jax.random.fold_in(own_key, axis), (), 0, length) for axis, length in enumerate(values.shape)]
        where[longest] = (where[longest] + shift) % values.shape[longest]
        spots.append(tuple(where))
    return values.at[spots[0]].set(smallest).at[spots[1]].set(top_value)


def block_scale(key, extent, pieces, smallest, top_value):
    factor_of = 1.0
    for axis_at, shards_of in pieces:
        draws = jax.random.uniform(jax.random.fold_in(jax.random.fold_in(key, 6), axis_at), (shards_of,), jnp.float32, smallest / len(pieces), top_value / len(pieces))
        factor_of = factor_of * jnp.repeat(jnp.exp(draws), extent[axis_at] // shards_of).reshape((-1,) + (1,) * (len(extent) - 1 - axis_at))
    return factor_of


def routed_block(key, own, number, rows, amount, top, limit, lean):
    sequence = jax.random.permutation(key, amount)
    crowded, common = portions_of(amount, rows * top, limit, lean, True), portions_of(amount, rows * top, limit, lean, False)
    places = jnp.arange(amount)

    def named(tallies, rotation):
        used = int((tallies > 0).sum())
        fixed = max(1, used // 4)
        passed = fixed + (places - fixed + rotation * (used - fixed)) % max(1, amount - fixed)
        return jnp.zeros((amount,), jnp.int32).at[sequence[jnp.where(places < fixed, places, passed)]].set(jnp.asarray(tallies, jnp.int32))

    tallies = jnp.where(number % 4 == 0, named(crowded, number // 4), named(common, number - number // 4 - 1))
    mixed = jax.random.permutation(jax.random.fold_in(own, 3), amount)
    giver, receiver = mixed[0:amount // 2 * 2:2], mixed[1:amount // 2 * 2:2]
    margin = jnp.minimum(tallies[giver] - 1, limit - tallies[receiver]) // 2
    margin = jnp.where((giver == sequence[0]) | (receiver == sequence[0]) | (tallies[receiver] == 0), 0, jnp.maximum(margin, 0))
    passed = jax.random.randint(jax.random.fold_in(own, 4), (amount // 2,), 0, 1 << 20) % (margin + 1)
    tallies = tallies.at[giver].add(-passed).at[receiver].add(passed)
    labels = jnp.searchsorted(jnp.cumsum(tallies), jnp.arange(rows * top), side="right").astype(jnp.int32)
    grid = labels.reshape(top, rows).T
    grid = grid[jax.random.permutation(jax.random.fold_in(own, 1), rows)]
    rotation = jax.random.randint(jax.random.fold_in(own, 2), (rows, 1), 0, top)
    return jnp.take_along_axis(grid, (jnp.arange(top)[None, :] + rotation) % top, axis=1)


def portions_of(number_of, total, bound, skew, full):
    weights = [(1 << 20) // math.isqrt(standing ** skew) + 1 for standing in range(1, number_of + 1)]
    largest = bound if full else min(bound, max(-(-total // number_of), total * weights[0] // sum(weights)))
    least = 1 if total - largest >= number_of - 1 else 0
    counts, rest = [largest] + [least] * (number_of - 1), total - largest - least * (number_of - 1)
    while rest > 0:
        candidates = [i for i in range(1, number_of) if counts[i] < largest] or [i for i in range(1, number_of) if counts[i] < bound]
        mass, remaining = sum([weights[i] for i in candidates]), rest
        for i in candidates:
            more = min(bound - counts[i], max(1, remaining * weights[i] // mass), rest)
            counts[i] = counts[i] + more
            rest = rest - more
    return np.array(counts)


def centred(own_key, extent, width, bound, cuts=(), kind=jnp.bfloat16):
    result = width * jax.random.normal(own_key, extent, jnp.float32)
    if cuts:
        result = result * block_scale(own_key, extent, cuts, -0.22, 0.18)
    return jnp.clip(result, -bound, bound).astype(kind)


def setup_inputs(seed: int = 0, part: int = 0) -> dict:
    key_of = jax.random.split(jax.random.key(seed), 8)
    part_keys = jax.random.split(jax.random.fold_in(key_of[7], part), 8)
    tokens = centred(part_keys[0], (TOKENS, D), 1.0, 6.0, ((0, 32),))
    targets = centred(part_keys[1], (TOKENS, D), 1.0, 6.0, ((0, 32),))
    expert_ids_keys = jax.random.split(jax.random.fold_in(part_keys[2], 1), TOKENS // TOK_DEV)
    expert_ids_turns = jax.random.permutation(jax.random.fold_in(part_keys[2], 3), TOKENS // TOK_DEV)
    expert_ids = jax.vmap(lambda own, number: routed_block(jax.random.fold_in(part_keys[2], 2), own, number, TOK_DEV, EXPERTS, TOP, MOST, 2))(expert_ids_keys, expert_ids_turns).reshape((TOKENS, TOP))
    gate_codes = touch_ends(jax.random.randint(part_keys[3], (TOKENS, TOP), 1, 256), jax.random.fold_in(part_keys[3], 1), 1, 255).astype(jnp.int32)
    projections = centred(key_of[4], (EXPERTS, 2, D, FF), D ** -0.5, 0.125, ((0, 16), (3, 2)))
    down_weight = centred(key_of[5], (EXPERTS, FF, D), FF ** -0.5, 0.21875, ((0, 16), (1, 2)))
    direction = centred(key_of[6], (EXPERTS, D, FF), D ** -0.5, 0.125, ((0, 16), (2, 2)))
    return {"tokens": tokens, "targets": targets, "expert_ids": expert_ids, "gate_codes": gate_codes, "projections": projections, "down_weight": down_weight, "direction": direction}


def slot_tables(route_ids, expert_total, slot_cap):
    routed_flat = route_ids.reshape(-1)
    route_count = routed_flat.shape[0]
    onehot = (routed_flat[:, None] == jnp.arange(expert_total, dtype=jnp.int32)[None, :]).astype(jnp.int32)
    earlier = jnp.cumsum(onehot, axis=0) - onehot
    within_slot = lax.optimization_barrier(jnp.sum(earlier * onehot, axis=1))
    landing = (routed_flat * slot_cap + within_slot).astype(jnp.int32)
    source_route = jnp.zeros((expert_total * slot_cap,), jnp.int32).at[landing].set(jnp.arange(route_count, dtype=jnp.int32))
    occupied = jnp.zeros((expert_total * slot_cap,), jnp.int32).at[landing].set(1)
    return (landing, source_route, occupied)

def slopes(gate_pre):
    sigmoid_val = jax.nn.sigmoid(gate_pre)
    first_slope = sigmoid_val * (1.0 + gate_pre * (1.0 - sigmoid_val))
    second_slope = sigmoid_val * (1.0 - sigmoid_val) * (2.0 + gate_pre * (1.0 - 2.0 * sigmoid_val))
    return (sigmoid_val, first_slope, second_slope)

def to_half(values):
    return lax.optimization_barrier(values.astype(jnp.bfloat16)).astype(jnp.float32)

def reference(tokens, targets, expert_ids, gate_codes, projections, down_weight, direction):
    dev_count = TOKENS // TOK_DEV
    slot_count = EXPERTS * MOST
    block_ids = expert_ids.reshape(dev_count, TOK_DEV, TOP)
    landing, source_route, occupied = jax.vmap(partial(slot_tables, expert_total=EXPERTS, slot_cap=MOST))(block_ids)
    token_blocks = tokens.reshape(dev_count, TOK_DEV, D)

    def place_rows(block_rows, route_index, filled):
        return jnp.where(filled[:, None] > 0, block_rows[route_index // TOP], jnp.zeros((), block_rows.dtype))
    send_rows = jax.vmap(place_rows)(token_blocks, source_route, occupied)
    slot_grid = send_rows.reshape(N_EXPERT, N_DP, N_EXPERT, EXP_DEV, MOST, D)

    def preacts(expert_index):
        arrived = slot_grid[:, :, expert_index].astype(jnp.float32)
        first_expert = expert_index * EXP_DEV
        pair_weight = lax.dynamic_slice_in_dim(projections, first_expert, EXP_DEV, 0).astype(jnp.float32)
        tangent_weight = lax.dynamic_slice_in_dim(direction, first_expert, EXP_DEV, 0).astype(jnp.float32)
        down_slice = lax.dynamic_slice_in_dim(down_weight, first_expert, EXP_DEV, 0).astype(jnp.float32)
        pair_pre = jnp.einsum('spxcd,xkdf->kspxcf', arrived, pair_weight)
        tangent_pre = jnp.einsum('spxcd,xdf->spxcf', arrived, tangent_weight)
        return (arrived, pair_pre[0], pair_pre[1], tangent_pre, down_slice)

    def forward_out(expert_index):
        arrived, gate_pre, up_pre, tangent_pre, down_slice = preacts(expert_index)
        sigmoid_val, first_slope, second_slope = slopes(gate_pre)
        hidden = to_half(gate_pre * sigmoid_val * up_pre)
        hidden_tan = to_half(first_slope * tangent_pre * up_pre)
        stacked_hidden = jnp.stack([hidden, hidden_tan])
        return jnp.einsum('kspxcf,xfd->kspxcd', stacked_hidden, down_slice).astype(jnp.bfloat16)
    expert_outputs = lax.map(forward_out, jnp.arange(N_EXPERT, dtype=jnp.int32))
    slot_out = jnp.transpose(expert_outputs, (2, 3, 1, 0, 4, 5, 6)).reshape(dev_count, 2, slot_count, D)
    route_weight = gate_codes.reshape(dev_count, TOK_DEV * TOP).astype(jnp.float32) / 256.0
    target_blocks = targets.reshape(dev_count, TOK_DEV, D)

    def combine(block_out, block_landing, block_weight, block_target, block_source, block_filled):
        route_out = block_out[:, block_landing].astype(jnp.float32)
        combined = lax.optimization_barrier(jnp.sum((route_out * block_weight[None, :, None]).reshape(2, TOK_DEV, TOP, D), axis=2))
        residual = combined[0] - block_target.astype(jnp.float32)
        pair_res = jnp.stack([residual, combined[1]])
        slot_weight = jnp.where(block_filled > 0, block_weight[block_source], jnp.zeros((), jnp.float32))
        return (pair_res[:, block_source // TOP] * slot_weight[None, :, None]).astype(jnp.bfloat16)
    outgoing = jax.vmap(combine)(slot_out, landing, route_weight, target_blocks, source_route, occupied)
    back_grid = outgoing.reshape(N_EXPERT, N_DP, 2, N_EXPERT, EXP_DEV, MOST, D)
    loss_scale = 1.0 / math.sqrt(TOK_DEV * TOP)

    def hessian_part(expert_index):
        arrived, gate_pre, up_pre, tangent_pre, down_slice = preacts(expert_index)
        sigmoid_val, first_slope, second_slope = slopes(gate_pre)
        incoming = back_grid[:, :, :, expert_index].astype(jnp.float32)
        grad_hidden = jnp.einsum('spkxcd,xfd->kspxcf', incoming, down_slice)
        hess_pre = to_half(grad_hidden[1] * up_pre * first_slope + grad_hidden[0] * up_pre * second_slope * tangent_pre)
        partial_sum = jnp.einsum('spxcd,spxcf->pxdf', arrived, hess_pre)
        rounded = to_half(partial_sum)
        return (lax.optimization_barrier(jnp.sum(rounded, axis=0)) * loss_scale).astype(jnp.bfloat16)
    hvp = lax.map(hessian_part, jnp.arange(N_EXPERT, dtype=jnp.int32))
    return hvp.reshape(EXPERTS, D, FF)
```

```python
import functools
import math

import jax
import jax.numpy as jnp
from jax import lax
from jax.experimental import pallas as pl
from jax.experimental.pallas import tpu as pltpu
from jax.sharding import PartitionSpec as P

LINE = 4
VMEM_BYTES = 56 * 1024 * 1024
DENSE_BYTES = 16 * 1024 * 1024


class Place:
    def __init__(self):
        expert = lax.axis_index("expert")
        self.z = expert // 4
        self.y = lax.rem(expert // 2, 2)
        self.c = lax.rem(expert, 2)
        self.x = lax.axis_index("dp")

    def line(self, d):
        return lax.rem(self.z + d, LINE)

    def device(self, z, y, c, x):
        return {"expert": (z * 2 + y) * 2 + c, "dp": x}

    def along_z(self, d):
        return self.device(self.line(d), self.y, self.c, self.x)

    def along_y(self):
        return self.device(self.z, 1 - self.y, self.c, self.x)

    def along_x(self):
        return self.device(self.z, self.y, self.c, 1 - self.x)

    def sibling(self):
        return self.device(self.z, self.y, 1 - self.c, self.x)

    def greet(self):
        barrier = pltpu.get_barrier_semaphore()
        others = [self.along_z(d) for d in range(1, LINE)]
        others += [self.along_y(), self.along_x(), self.sibling()]
        for other in others:
            pl.semaphore_signal(
                barrier, inc=1, device_id=other, device_id_type=pl.DeviceIdType.MESH
            )
        pl.semaphore_wait(barrier, len(others))


def remote(src, dst, send_sem, recv_sem, to):
    return pltpu.make_async_remote_copy(
        src_ref=src,
        dst_ref=dst,
        send_sem=send_sem,
        recv_sem=recv_sem,
        device_id=to,
        device_id_type=pl.DeviceIdType.MESH,
    )


def spread(me, pieces, send_sem, recv_sem):
    sends = []

    def copy(p, block, to, number):
        ref = pieces[p][0](*block)
        return remote(ref, ref, send_sem.at[number], recv_sem.at[(p,) + block], to)

    def push(p, block, to):
        item = copy(p, block, to, len(sends))
        item.start()
        sends.append(item)

    def arrive(p, block):
        copy(p, block, me.sibling(), 0).wait_recv()

    count = range(len(pieces))
    ways = [
        (me.along_y(), me.along_x()) if first == "y" else (me.along_x(), me.along_y())
        for _, first in pieces
    ]
    own = (me.z, me.y, me.c, me.x)
    for d in (2, 1, 3):
        for p in count:
            push(p, own, me.along_z(d))
    for d in range(LINE):
        z = me.line(d)
        for p in count:
            block = (z, me.y, me.c, me.x)
            if d:
                arrive(p, block)
            push(p, block, ways[p][0])
            push(p, block, ways[p][1])
            push(p, block, me.sibling())
        for p in count:
            y_first = pieces[p][1] == "y"
            block = (z, 1 - me.y, me.c, me.x) if y_first else (z, me.y, me.c, 1 - me.x)
            arrive(p, block)
            push(p, block, ways[p][1])
            push(p, block, me.sibling())
    for d in range(LINE):
        z = me.line(d)
        for p in count:
            y_first = pieces[p][1] == "y"
            near = (z, me.y, me.c, 1 - me.x) if y_first else (z, 1 - me.y, me.c, me.x)
            for block in (near, (z, 1 - me.y, me.c, 1 - me.x)):
                arrive(p, block)
                push(p, block, me.sibling())
    for d in range(LINE):
        for p in count:
            for y in range(2):
                for x in range(2):
                    arrive(p, (me.line(d), y, 1 - me.c, x))
    for item in sends:
        item.wait_send()


SPREAD_SENDS = 3 + LINE * 5 + LINE * 2


def gather_kernel(tok_ref, weight_ref, all_tok, all_weight, send_sem, recv_sem):
    me = Place()
    half = tok_ref.shape[1] // 2
    all_tok[me.z, me.y, me.c, me.x] = tok_ref[...]
    all_weight[me.z, me.y, me.c, me.x] = weight_ref[...]
    me.greet()
    pieces = [
        (lambda z, y, c, x: all_tok.at[z, y, c, x, :, pl.ds(0, half)], "y"),
        (lambda z, y, c, x: all_tok.at[z, y, c, x, :, pl.ds(half, half)], "x"),
        (lambda z, y, c, x: all_weight.at[z, y, c, x], "y"),
    ]
    spread(me, pieces, send_sem, recv_sem)


def gather_tokens(tokens, weights):
    rows, width = tokens.shape
    grid = (LINE, 2, 2, 2)
    vmem = pl.BlockSpec(memory_space=pltpu.VMEM)
    return pl.pallas_call(
        gather_kernel,
        out_shape=(
            jax.ShapeDtypeStruct(grid + (rows, width), tokens.dtype),
            jax.ShapeDtypeStruct(grid + weights.shape, weights.dtype),
        ),
        in_specs=[vmem] * 2,
        out_specs=(vmem, vmem),
        scratch_shapes=[
            pltpu.SemaphoreType.DMA((3 * SPREAD_SENDS,)),
            pltpu.SemaphoreType.DMA((3,) + grid),
        ],
        compiler_params=pltpu.CompilerParams(
            collective_id=0, has_side_effects=True, vmem_limit_bytes=VMEM_BYTES
        ),
    )(tokens, weights)


def exchange_kernel(
    part, targets, out, core_in, out1, in1, out2, in2, out3, in3,
    core_send, core_recv, send1, recv1, send2, recv2, send3, recv3, send_sem, recv_sem,
):
    me = Place()
    half = targets.shape[1] // 2
    me.greet()
    sends = []

    def push(src, dst, send, recv, to):
        item = remote(src, dst, send, recv, to)
        item.start()
        sends.append(item)
        return item

    turn = (1, 2, 3, 0)
    core_copies = {}
    for d in turn:
        z = me.line(d)
        core_copies[d] = push(
            part.at[:, z, :, 1 - me.c], core_in.at[:, z], core_send.at[d], core_recv.at[d],
            me.sibling(),
        )

    def pair(h, z, far, near):
        cols = pl.ds(h * half, half)
        y, x = (near, far) if h == 0 else (far, near)
        mine = part[:, z, y, me.c, x, :, cols].astype(jnp.float32)
        return mine + core_in[:, z, y, x, :, cols].astype(jnp.float32)

    axis1 = (me.along_x(), me.along_y())
    axis2 = (me.along_y(), me.along_x())
    far_own = (me.x, me.y)
    near_own = (me.y, me.x)
    first, second, third = {}, {}, {}
    for d in turn:
        z = me.line(d)
        core_copies[d].wait_recv()
        for h in range(2):
            for near in range(2):
                out1[h, d, near] = pair(h, z, 1 - far_own[h], near).astype(out1.dtype)
            first[d, h] = push(
                out1.at[h, d], in1.at[h, d], send1.at[h, d], recv1.at[h, d], axis1[h]
            )
    for d in turn:
        z = me.line(d)
        for h in range(2):
            first[d, h].wait_recv()
            near = 1 - near_own[h]
            total = pair(h, z, far_own[h], near) + in1[h, d, near].astype(jnp.float32)
            out2[h, d] = total.astype(out2.dtype)
            second[d, h] = push(
                out2.at[h, d], in2.at[h, d], send2.at[h, d], recv2.at[h, d], axis2[h]
            )
    held = [None, None]
    for d in turn:
        z = me.line(d)
        for h in range(2):
            second[d, h].wait_recv()
            near = near_own[h]
            total = pair(h, z, far_own[h], near) + in1[h, d, near].astype(jnp.float32)
            total = total + in2[h, d].astype(jnp.float32)
            if d:
                out3[h, d - 1] = total.astype(out3.dtype)
                third[d, h] = push(
                    out3.at[h, d - 1], in3.at[h, d - 1], send3.at[h, d - 1], recv3.at[h, d - 1],
                    me.along_z(d),
                )
            else:
                held[h] = total
    for h in range(2):
        cols = pl.ds(h * half, half)
        total = held[h]
        for d in range(1, LINE):
            third[d, h].wait_recv()
            total = total + in3[h, d - 1].astype(jnp.float32)
        residual = total[0] - targets[:, cols].astype(jnp.float32)
        out[0, me.z, me.y, me.c, me.x, :, cols] = residual.astype(out.dtype)
        out[1, me.z, me.y, me.c, me.x, :, cols] = total[1].astype(out.dtype)
    pieces = [
        (lambda z, y, c, x: out.at[:, z, y, c, x, :, pl.ds(0, half)], "y"),
        (lambda z, y, c, x: out.at[:, z, y, c, x, :, pl.ds(half, half)], "x"),
    ]
    spread(me, pieces, send_sem, recv_sem)
    for item in sends:
        item.wait_send()


def exchange(part, targets):
    rows, width = targets.shape
    half = width // 2
    grid = (LINE, 2, 2, 2)
    kind = part.dtype
    vmem = pl.BlockSpec(memory_space=pltpu.VMEM)
    dma = pltpu.SemaphoreType.DMA
    return pl.pallas_call(
        exchange_kernel,
        out_shape=jax.ShapeDtypeStruct((2,) + grid + (rows, width), kind),
        in_specs=[vmem] * 2,
        out_specs=vmem,
        scratch_shapes=[
            pltpu.VMEM((2, LINE, 2, 2, rows, width), kind),
            pltpu.VMEM((2, LINE, 2, 2, rows, half), kind),
            pltpu.VMEM((2, LINE, 2, 2, rows, half), kind),
            pltpu.VMEM((2, LINE, 2, rows, half), kind),
            pltpu.VMEM((2, LINE, 2, rows, half), kind),
            pltpu.VMEM((2, LINE - 1, 2, rows, half), kind),
            pltpu.VMEM((2, LINE - 1, 2, rows, half), kind),
            dma((LINE,)),
            dma((LINE,)),
            dma((2, LINE)),
            dma((2, LINE)),
            dma((2, LINE)),
            dma((2, LINE)),
            dma((2, LINE - 1)),
            dma((2, LINE - 1)),
            dma((2 * SPREAD_SENDS,)),
            dma((2,) + grid),
        ],
        compiler_params=pltpu.CompilerParams(
            collective_id=1, has_side_effects=True, vmem_limit_bytes=VMEM_BYTES
        ),
    )(part, targets)


def dense_body(tokens, targets, expert_ids, gate_codes, projections, down_weight, direction):
    tok_rows, model_width = tokens.shape
    top_count = expert_ids.shape[1]
    expert = lax.axis_index("expert")
    lanes = jnp.arange(128, dtype=jnp.int32)
    named = expert_ids[:, :, None] == lanes[None, None, :]
    table = jnp.sum(jnp.where(named, gate_codes[:, :, None], 0), axis=1)
    table = (table.astype(jnp.float32) / 256.0).astype(jnp.bfloat16)
    all_tok, all_table = gather_tokens(tokens, table)
    grid = all_tok.shape[:4]
    all_tok = all_tok.reshape(-1, model_width)
    weight = jnp.sum(
        jnp.where(lanes[None, :] == expert, all_table.reshape(-1, 128).astype(jnp.float32), 0.0),
        axis=1,
        keepdims=True,
    )
    dot = functools.partial(jnp.einsum, preferred_element_type=jnp.float32)
    gate_pre = dot("td,df->tf", all_tok, projections[0, 0])
    up_pre = dot("td,df->tf", all_tok, projections[0, 1])
    tangent_pre = dot("td,df->tf", all_tok, direction[0])
    sigmoid_val = jax.nn.sigmoid(gate_pre)
    first_slope = sigmoid_val * (1.0 + gate_pre * (1.0 - sigmoid_val))
    second_slope = sigmoid_val * (1.0 - sigmoid_val) * (2.0 + gate_pre * (1.0 - 2.0 * sigmoid_val))
    hidden = (weight * gate_pre * sigmoid_val * up_pre).astype(jnp.bfloat16)
    hidden_tan = (weight * first_slope * tangent_pre * up_pre).astype(jnp.bfloat16)
    part = dot("ktf,fd->ktd", jnp.stack([hidden, hidden_tan]), down_weight[0])
    part = part.astype(jnp.bfloat16).reshape((2,) + grid + (tok_rows, model_width))
    back = exchange(part, targets).reshape(2, -1, model_width)
    grad = dot("ktd,fd->ktf", back, down_weight[0])
    hess_pre = (
        weight * (grad[1] * up_pre * first_slope + grad[0] * up_pre * second_slope * tangent_pre)
    ).astype(jnp.bfloat16)
    total = dot("td,tf->df", all_tok, hess_pre)
    loss_scale = 1.0 / math.sqrt(tok_rows * top_count)
    return (total * loss_scale).astype(jnp.bfloat16)[None]


def slot_tables(route_ids, expert_total, slot_cap):
    routed_flat = route_ids.reshape(-1)
    route_count = routed_flat.shape[0]
    onehot = (routed_flat[:, None] == jnp.arange(expert_total, dtype=jnp.int32)[None, :]).astype(
        jnp.int32
    )
    earlier = jnp.cumsum(onehot, axis=0) - onehot
    within_slot = jnp.sum(earlier * onehot, axis=1)
    landing = routed_flat * slot_cap + within_slot
    source_route = (
        jnp.zeros((expert_total * slot_cap,), jnp.int32)
        .at[landing]
        .set(jnp.arange(route_count, dtype=jnp.int32))
    )
    occupied = jnp.zeros((expert_total * slot_cap,), jnp.int32).at[landing].set(1)
    return (landing, source_route, occupied)


def routed_body(tokens, targets, expert_ids, gate_codes, projections, down_weight, direction):
    tok_rows, model_width = tokens.shape
    top_count = expert_ids.shape[1]
    local_experts = projections.shape[0]
    expert_devs = lax.axis_size("expert")
    all_experts = local_experts * expert_devs
    slot_cap = max(2, tok_rows * top_count // all_experts + 1)
    landing, source_route, occupied = slot_tables(expert_ids, all_experts, slot_cap)
    source_token = source_route // top_count
    send_rows = jnp.where(occupied[:, None] > 0, tokens[source_token], jnp.zeros((), tokens.dtype))
    send_rows = send_rows.reshape(expert_devs, local_experts, slot_cap, model_width)
    arrived = lax.all_to_all(send_rows, "expert", split_axis=0, concat_axis=0, tiled=True)
    pair_pre = jnp.einsum(
        "sxcd,xkdf->ksxcf",
        arrived,
        lax.all_gather(projections, "dp", axis=3, tiled=True),
        preferred_element_type=jnp.float32,
    )
    tangent_pre = jnp.einsum(
        "sxcd,xdf->sxcf",
        arrived,
        lax.all_gather(direction, "dp", axis=2, tiled=True),
        preferred_element_type=jnp.float32,
    )
    gate_pre = pair_pre[0]
    up_pre = pair_pre[1]
    down_full = lax.all_gather(down_weight, "dp", axis=1, tiled=True)
    sigmoid_val = jax.nn.sigmoid(gate_pre)
    first_slope = sigmoid_val * (1.0 + gate_pre * (1.0 - sigmoid_val))
    second_slope = sigmoid_val * (1.0 - sigmoid_val) * (2.0 + gate_pre * (1.0 - 2.0 * sigmoid_val))
    hidden = (gate_pre * sigmoid_val * up_pre).astype(jnp.bfloat16)
    hidden_tan = (first_slope * tangent_pre * up_pre).astype(jnp.bfloat16)
    stacked_hidden = jnp.stack([hidden, hidden_tan])
    expert_out = jnp.einsum(
        "ksxcf,xfd->ksxcd", stacked_hidden, down_full, preferred_element_type=jnp.float32
    ).astype(jnp.bfloat16)
    returned = lax.all_to_all(expert_out, "expert", split_axis=1, concat_axis=1, tiled=True)
    slot_out = returned.reshape(2, all_experts * slot_cap, model_width)
    route_out = slot_out[:, landing].astype(jnp.float32)
    route_weight = gate_codes.reshape(-1).astype(jnp.float32) / 256.0
    combined = jnp.sum(
        (route_out * route_weight[None, :, None]).reshape(2, tok_rows, top_count, model_width),
        axis=2,
    )
    residual = combined[0] - targets.astype(jnp.float32)
    pair_res = jnp.stack([residual, combined[1]])
    slot_weight = jnp.where(occupied > 0, route_weight[source_route], jnp.zeros((), jnp.float32))
    outgoing = (pair_res[:, source_token] * slot_weight[None, :, None]).astype(jnp.bfloat16)
    outgoing = outgoing.reshape(2, expert_devs, local_experts, slot_cap, model_width)
    incoming = lax.all_to_all(outgoing, "expert", split_axis=1, concat_axis=1, tiled=True)
    grad_hidden = jnp.einsum(
        "ksxcd,xfd->ksxcf", incoming, down_full, preferred_element_type=jnp.float32
    )
    hess_pre = (
        grad_hidden[1] * up_pre * first_slope + grad_hidden[0] * up_pre * second_slope * tangent_pre
    ).astype(jnp.bfloat16)
    partial_sum = jnp.einsum(
        "sxcd,sxcf->xdf", arrived, hess_pre, preferred_element_type=jnp.float32
    )
    summed = lax.psum_scatter(
        partial_sum.astype(jnp.bfloat16), "dp", scatter_dimension=2, tiled=True
    ).astype(jnp.float32)
    loss_scale = 1.0 / math.sqrt(tok_rows * top_count)
    return (summed * loss_scale).astype(jnp.bfloat16)


def plan(mesh):
    shape = dict(mesh.shape)
    fits = shape["groups"] == 1 and shape["expert"] == LINE * 4 and shape["dp"] == 2

    def body(tokens, targets, expert_ids, gate_codes, projections, down_weight, direction):
        everyone = shape["expert"] * shape["dp"] * tokens.size * tokens.dtype.itemsize
        dense = fits and projections.shape[0] == 1 and everyone * 2 <= DENSE_BYTES
        chosen = dense_body if dense else routed_body
        return chosen(
            tokens, targets, expert_ids, gate_codes, projections, down_weight, direction
        )

    return body


def solution(mesh):
    return jax.shard_map(
        plan(mesh),
        mesh=mesh,
        in_specs=(
            P(("groups", "expert", "dp"), None),
            P(("groups", "expert", "dp"), None),
            P(("groups", "expert", "dp"), None),
            P(("groups", "expert", "dp"), None),
            P("expert", None, None, "dp"),
            P("expert", "dp", None),
            P("expert", None, "dp"),
        ),
        out_specs=P(("groups", "expert"), None, "dp"),
        check_vma=False,
    )
```

```python
import functools
import math

import jax
import jax.numpy as jnp
from jax import lax
from jax.experimental import pallas as pl
from jax.experimental.pallas import tpu as pltpu
from jax.sharding import PartitionSpec as P

LINE = 4
VMEM_BYTES = 56 * 1024 * 1024
DENSE_BYTES = 16 * 1024 * 1024


class Place:
    def __init__(self):
        expert = lax.axis_index("expert")
        self.z = expert // 4
        self.y = lax.rem(expert // 2, 2)
        self.c = lax.rem(expert, 2)
        self.x = lax.axis_index("dp")

    def line(self, d):
        return lax.rem(self.z + d, LINE)

    def device(self, z, y, c, x):
        return {"expert": (z * 2 + y) * 2 + c, "dp": x}

    def along_z(self, d):
        return self.device(self.line(d), self.y, self.c, self.x)

    def along_y(self):
        return self.device(self.z, 1 - self.y, self.c, self.x)

    def along_x(self):
        return self.device(self.z, self.y, self.c, 1 - self.x)

    def sibling(self):
        return self.device(self.z, self.y, 1 - self.c, self.x)

    def greet(self):
        barrier = pltpu.get_barrier_semaphore()
        others = [self.along_z(d) for d in range(1, LINE)]
        others += [self.along_y(), self.along_x(), self.sibling()]
        for other in others:
            pl.semaphore_signal(
                barrier, inc=1, device_id=other, device_id_type=pl.DeviceIdType.MESH
            )
        pl.semaphore_wait(barrier, len(others))


def remote(src, dst, send_sem, recv_sem, to):
    return pltpu.make_async_remote_copy(
        src_ref=src,
        dst_ref=dst,
        send_sem=send_sem,
        recv_sem=recv_sem,
        device_id=to,
        device_id_type=pl.DeviceIdType.MESH,
    )


class Spread:
    def __init__(self, me, pieces, send_sem, recv_sem):
        self.me, self.pieces = me, pieces
        self.send_sem, self.recv_sem = send_sem, recv_sem
        self.sends = []
        self.ways = [
            (me.along_y(), me.along_x()) if first == "y" else (me.along_x(), me.along_y())
            for _, first in pieces
        ]

    def copy(self, p, block, to, number):
        ref = self.pieces[p][0](*block)
        return remote(ref, ref, self.send_sem.at[number], self.recv_sem.at[(p,) + block], to)

    def push(self, p, block, to):
        item = self.copy(p, block, to, len(self.sends))
        item.start()
        self.sends.append(item)

    def arrive(self, p, block):
        self.copy(p, block, self.me.sibling(), 0).wait_recv()

    def blocks(self, p, d):
        me, z = self.me, self.me.line(d)
        own = (z, me.y, me.c, me.x)
        by_y = (z, 1 - me.y, me.c, me.x)
        by_x = (z, me.y, me.c, 1 - me.x)
        both = (z, 1 - me.y, me.c, 1 - me.x)
        return (own, by_y, by_x, both) if self.pieces[p][1] == "y" else (own, by_x, by_y, both)

    def start(self):
        for d in range(LINE - 1, 0, -1):
            for p in range(len(self.pieces)):
                self.push(p, self.blocks(p, 0)[0], self.me.along_z(d))

    def line_step(self, d):
        for p in range(len(self.pieces)):
            block = self.blocks(p, d)[0]
            if d:
                self.arrive(p, block)
            self.push(p, block, self.ways[p][0])
            self.push(p, block, self.ways[p][1])
            self.push(p, block, self.me.sibling())

    def first_step(self, d):
        for p in range(len(self.pieces)):
            block = self.blocks(p, d)[1]
            self.arrive(p, block)
            self.push(p, block, self.ways[p][1])
            self.push(p, block, self.me.sibling())

    def second_step(self, d):
        for p in range(len(self.pieces)):
            for block in self.blocks(p, d)[2:]:
                self.arrive(p, block)
                self.push(p, block, self.me.sibling())

    def core_step(self, d):
        for p in range(len(self.pieces)):
            for y in range(2):
                for x in range(2):
                    self.arrive(p, (self.me.line(d), y, 1 - self.me.c, x))

    def finish(self):
        for item in self.sends:
            item.wait_send()


SPREAD_SENDS = 3 + LINE * 5 + LINE * 2


def rows_of(block):
    return block.reshape(-1, block.shape[-1])


def dot(a, b, dims=((1,), (0,))):
    return lax.dot_general(a, b, (dims, ((), ())), preferred_element_type=jnp.float32)


def fused_kernel(
    loss_scale, tok_ref, table_ref, targets, proj_hbm, down_hbm, dir_hbm, hvp_ref,
    all_tok, all_table, proj, down, direction, slope_a, slope_b,
    part, back, total_hvp, core_in, out1, in1, out2, in2, out3, in3,
    weight_sem, core_send, core_recv, send1, recv1, send2, recv2, send3, recv3,
    tok_send, tok_recv, back_send, back_recv,
):
    me = Place()
    expert = lax.axis_index("expert")
    half = tok_ref.shape[1] // 2
    loads = [
        pltpu.make_async_copy(proj_hbm.at[0], proj, weight_sem.at[0]),
        pltpu.make_async_copy(dir_hbm.at[0], direction, weight_sem.at[1]),
        pltpu.make_async_copy(down_hbm.at[0], down, weight_sem.at[2]),
    ]
    for load in loads:
        load.start()
    all_tok[me.z, me.y, me.c, me.x] = tok_ref[...]
    all_table[me.z, me.y, me.c, me.x] = table_ref[...]
    me.greet()
    tok = Spread(
        me,
        [
            (lambda z, y, c, x: all_tok.at[z, y, c, x, :, pl.ds(0, half)], "y"),
            (lambda z, y, c, x: all_tok.at[z, y, c, x, :, pl.ds(half, half)], "x"),
            (lambda z, y, c, x: all_table.at[z, y, c, x], "y"),
        ],
        tok_send,
        tok_recv,
    )
    sends = []

    def push(src, dst, send, recv, to):
        item = remote(src, dst, send, recv, to)
        item.start()
        sends.append(item)
        return item

    def forward(d):
        z = me.line(d)
        rows = rows_of(all_tok[z])
        gate_pre = dot(rows, proj[0])
        up_pre = dot(rows, proj[1])
        tangent_pre = dot(rows, direction[...])
        table = rows_of(all_table[z].astype(jnp.float32))
        named = lax.broadcasted_iota(jnp.int32, table.shape, 1) == expert
        weight = jnp.sum(jnp.where(named, table, 0.0), axis=1, keepdims=True)
        sig = jax.nn.sigmoid(gate_pre)
        rest = 1.0 - sig
        up_weighted = weight * up_pre
        slope = up_weighted * (sig * (1.0 + gate_pre * rest))
        curve = up_weighted * (sig * rest * (2.0 + gate_pre * (1.0 - 2.0 * sig))) * tangent_pre
        slope_a[d] = slope
        slope_b[d] = curve
        hidden = (gate_pre * sig * up_weighted).astype(jnp.bfloat16)
        hidden_tan = (slope * tangent_pre).astype(jnp.bfloat16)
        if d == 0:
            loads[2].wait()
        for k, value in enumerate((hidden, hidden_tan)):
            out = dot(value, down[...]).reshape(part.shape[2:])
            part[k, z] = out.astype(part.dtype)

    core_copies, first, second, third = {}, {}, {}, {}

    def core_send_step(d):
        z = me.line(d)
        core_copies[d] = push(
            part.at[:, z, :, 1 - me.c], core_in.at[:, z], core_send.at[d], core_recv.at[d],
            me.sibling(),
        )

    def pair(h, z, far, near):
        cols = pl.ds(h * half, half)
        y, x = (near, far) if h == 0 else (far, near)
        mine = part[:, z, y, me.c, x, :, cols].astype(jnp.float32)
        return mine + core_in[:, z, y, x, :, cols].astype(jnp.float32)

    axis1 = (me.along_x(), me.along_y())
    axis2 = (me.along_y(), me.along_x())
    far_own = (me.x, me.y)
    near_own = (me.y, me.x)

    def sum_first(d):
        core_copies[d].wait_recv()
        for h in range(2):
            for near in range(2):
                out1[h, d, near] = pair(h, me.line(d), 1 - far_own[h], near).astype(out1.dtype)
            first[d, h] = push(
                out1.at[h, d], in1.at[h, d], send1.at[h, d], recv1.at[h, d], axis1[h]
            )

    def sum_second(d):
        for h in range(2):
            first[d, h].wait_recv()
            near = 1 - near_own[h]
            total = pair(h, me.line(d), far_own[h], near) + in1[h, d, near].astype(jnp.float32)
            out2[h, d] = total.astype(out2.dtype)
            second[d, h] = push(
                out2.at[h, d], in2.at[h, d], send2.at[h, d], recv2.at[h, d], axis2[h]
            )

    def plane_total(d, h):
        second[d, h].wait_recv()
        near = near_own[h]
        total = pair(h, me.line(d), far_own[h], near) + in1[h, d, near].astype(jnp.float32)
        return total + in2[h, d].astype(jnp.float32)

    def sum_third(d):
        for h in range(2):
            out3[h, d - 1] = plane_total(d, h).astype(out3.dtype)
            third[d, h] = push(
                out3.at[h, d - 1], in3.at[h, d - 1], send3.at[h, d - 1], recv3.at[h, d - 1],
                me.along_z(d),
            )

    tok.start()
    tok.line_step(0)
    tok.first_step(0)
    tok.line_step(1)
    tok.second_step(0)
    tok.first_step(1)
    tok.core_step(0)
    loads[0].wait()
    loads[1].wait()
    forward(0)
    core_send_step(0)
    tok.line_step(2)
    tok.second_step(1)
    tok.first_step(2)
    tok.core_step(1)
    sum_first(0)
    tok.line_step(3)
    forward(1)
    core_send_step(1)
    tok.first_step(3)
    tok.second_step(2)
    tok.core_step(2)
    sum_first(1)
    sum_second(0)
    forward(2)
    core_send_step(2)
    tok.second_step(3)
    tok.core_step(3)
    sum_first(2)
    sum_second(1)
    forward(3)
    core_send_step(3)
    sum_third(1)
    sum_first(3)
    sum_second(2)
    sum_third(2)
    sum_second(3)
    sum_third(3)

    spread = Spread(
        me,
        [
            (lambda z, y, c, x: back.at[:, z, y, c, x, :, pl.ds(0, half)], "y"),
            (lambda z, y, c, x: back.at[:, z, y, c, x, :, pl.ds(half, half)], "x"),
        ],
        back_send,
        back_recv,
    )
    for h in range(2):
        cols = pl.ds(h * half, half)
        total = plane_total(0, h)
        for d in range(1, LINE):
            third[d, h].wait_recv()
            total = total + in3[h, d - 1].astype(jnp.float32)
        residual = total[0] - targets[:, cols].astype(jnp.float32)
        back[0, me.z, me.y, me.c, me.x, :, cols] = residual.astype(back.dtype)
        back[1, me.z, me.y, me.c, me.x, :, cols] = total[1].astype(back.dtype)

    def backward(d):
        z = me.line(d)
        grad_hidden = dot(rows_of(back[0, z]), down[...], ((1,), (1,)))
        grad_tangent = dot(rows_of(back[1, z]), down[...], ((1,), (1,)))
        hess_pre = (grad_tangent * slope_a[d] + grad_hidden * slope_b[d]).astype(jnp.bfloat16)
        term = dot(rows_of(all_tok[z]), hess_pre, ((0,), (0,)))
        if d == 0:
            total_hvp[...] = term
        elif d < LINE - 1:
            total_hvp[...] += term
        else:
            hvp_ref[0] = ((total_hvp[...] + term) * loss_scale).astype(hvp_ref.dtype)

    spread.start()
    spread.line_step(0)
    spread.first_step(0)
    spread.line_step(1)
    spread.second_step(0)
    spread.first_step(1)
    spread.core_step(0)
    spread.line_step(2)
    backward(0)
    spread.second_step(1)
    spread.first_step(2)
    spread.core_step(1)
    spread.line_step(3)
    backward(1)
    spread.first_step(3)
    spread.second_step(2)
    spread.core_step(2)
    backward(2)
    spread.second_step(3)
    spread.core_step(3)
    backward(3)
    tok.finish()
    spread.finish()
    for item in sends:
        item.wait_send()


def dense_body(tokens, targets, expert_ids, gate_codes, projections, down_weight, direction):
    rows, width = tokens.shape
    units = down_weight.shape[1]
    top_count = expert_ids.shape[1]
    half = width // 2
    grid = (LINE, 2, 2, 2)
    plane_rows = 8 * rows
    kind = tokens.dtype
    lanes = jnp.arange(128, dtype=jnp.int32)
    named = expert_ids[:, :, None] == lanes[None, None, :]
    table = jnp.sum(jnp.where(named, gate_codes[:, :, None], 0), axis=1)
    table = (table.astype(jnp.float32) / 256.0).astype(jnp.bfloat16)
    vmem = pl.BlockSpec(memory_space=pltpu.VMEM)
    hbm = pl.BlockSpec(memory_space=pl.ANY)
    dma = pltpu.SemaphoreType.DMA
    return pl.pallas_call(
        functools.partial(fused_kernel, 1.0 / math.sqrt(rows * top_count)),
        out_shape=jax.ShapeDtypeStruct((1, width, units), jnp.bfloat16),
        in_specs=[vmem] * 3 + [hbm] * 3,
        out_specs=vmem,
        scratch_shapes=[
            pltpu.VMEM(grid + (rows, width), kind),
            pltpu.VMEM(grid + (rows, 128), kind),
            pltpu.VMEM((2, width, units), kind),
            pltpu.VMEM((units, width), kind),
            pltpu.VMEM((width, units), kind),
            pltpu.VMEM((LINE, plane_rows, units), jnp.float32),
            pltpu.VMEM((LINE, plane_rows, units), jnp.float32),
            pltpu.VMEM((2,) + grid + (rows, width), kind),
            pltpu.VMEM((2,) + grid + (rows, width), kind),
            pltpu.VMEM((width, units), jnp.float32),
            pltpu.VMEM((2, LINE, 2, 2, rows, width), kind),
            pltpu.VMEM((2, LINE, 2, 2, rows, half), kind),
            pltpu.VMEM((2, LINE, 2, 2, rows, half), kind),
            pltpu.VMEM((2, LINE, 2, rows, half), kind),
            pltpu.VMEM((2, LINE, 2, rows, half), kind),
            pltpu.VMEM((2, LINE - 1, 2, rows, half), kind),
            pltpu.VMEM((2, LINE - 1, 2, rows, half), kind),
            dma((3,)),
            dma((LINE,)),
            dma((LINE,)),
            dma((2, LINE)),
            dma((2, LINE)),
            dma((2, LINE)),
            dma((2, LINE)),
            dma((2, LINE - 1)),
            dma((2, LINE - 1)),
            dma((3 * SPREAD_SENDS,)),
            dma((3,) + grid),
            dma((2 * SPREAD_SENDS,)),
            dma((2,) + grid),
        ],
        compiler_params=pltpu.CompilerParams(
            collective_id=0, has_side_effects=True, vmem_limit_bytes=VMEM_BYTES
        ),
    )(tokens, table, targets, projections, down_weight, direction)


def slot_tables(route_ids, expert_total, slot_cap):
    routed_flat = route_ids.reshape(-1)
    route_count = routed_flat.shape[0]
    onehot = (routed_flat[:, None] == jnp.arange(expert_total, dtype=jnp.int32)[None, :]).astype(
        jnp.int32
    )
    earlier = jnp.cumsum(onehot, axis=0) - onehot
    within_slot = jnp.sum(earlier * onehot, axis=1)
    landing = routed_flat * slot_cap + within_slot
    source_route = (
        jnp.zeros((expert_total * slot_cap,), jnp.int32)
        .at[landing]
        .set(jnp.arange(route_count, dtype=jnp.int32))
    )
    occupied = jnp.zeros((expert_total * slot_cap,), jnp.int32).at[landing].set(1)
    return (landing, source_route, occupied)


def routed_body(tokens, targets, expert_ids, gate_codes, projections, down_weight, direction):
    tok_rows, model_width = tokens.shape
    top_count = expert_ids.shape[1]
    local_experts = projections.shape[0]
    expert_devs = lax.axis_size("expert")
    all_experts = local_experts * expert_devs
    slot_cap = max(2, tok_rows * top_count // all_experts + 1)
    landing, source_route, occupied = slot_tables(expert_ids, all_experts, slot_cap)
    source_token = source_route // top_count
    send_rows = jnp.where(occupied[:, None] > 0, tokens[source_token], jnp.zeros((), tokens.dtype))
    send_rows = send_rows.reshape(expert_devs, local_experts, slot_cap, model_width)
    arrived = lax.all_to_all(send_rows, "expert", split_axis=0, concat_axis=0, tiled=True)
    pair_pre = jnp.einsum(
        "sxcd,xkdf->ksxcf",
        arrived,
        lax.all_gather(projections, "dp", axis=3, tiled=True),
        preferred_element_type=jnp.float32,
    )
    tangent_pre = jnp.einsum(
        "sxcd,xdf->sxcf",
        arrived,
        lax.all_gather(direction, "dp", axis=2, tiled=True),
        preferred_element_type=jnp.float32,
    )
    gate_pre = pair_pre[0]
    up_pre = pair_pre[1]
    down_full = lax.all_gather(down_weight, "dp", axis=1, tiled=True)
    sigmoid_val = jax.nn.sigmoid(gate_pre)
    first_slope = sigmoid_val * (1.0 + gate_pre * (1.0 - sigmoid_val))
    second_slope = sigmoid_val * (1.0 - sigmoid_val) * (2.0 + gate_pre * (1.0 - 2.0 * sigmoid_val))
    hidden = (gate_pre * sigmoid_val * up_pre).astype(jnp.bfloat16)
    hidden_tan = (first_slope * tangent_pre * up_pre).astype(jnp.bfloat16)
    stacked_hidden = jnp.stack([hidden, hidden_tan])
    expert_out = jnp.einsum(
        "ksxcf,xfd->ksxcd", stacked_hidden, down_full, preferred_element_type=jnp.float32
    ).astype(jnp.bfloat16)
    returned = lax.all_to_all(expert_out, "expert", split_axis=1, concat_axis=1, tiled=True)
    slot_out = returned.reshape(2, all_experts * slot_cap, model_width)
    route_out = slot_out[:, landing].astype(jnp.float32)
    route_weight = gate_codes.reshape(-1).astype(jnp.float32) / 256.0
    combined = jnp.sum(
        (route_out * route_weight[None, :, None]).reshape(2, tok_rows, top_count, model_width),
        axis=2,
    )
    residual = combined[0] - targets.astype(jnp.float32)
    pair_res = jnp.stack([residual, combined[1]])
    slot_weight = jnp.where(occupied > 0, route_weight[source_route], jnp.zeros((), jnp.float32))
    outgoing = (pair_res[:, source_token] * slot_weight[None, :, None]).astype(jnp.bfloat16)
    outgoing = outgoing.reshape(2, expert_devs, local_experts, slot_cap, model_width)
    incoming = lax.all_to_all(outgoing, "expert", split_axis=1, concat_axis=1, tiled=True)
    grad_hidden = jnp.einsum(
        "ksxcd,xfd->ksxcf", incoming, down_full, preferred_element_type=jnp.float32
    )
    hess_pre = (
        grad_hidden[1] * up_pre * first_slope + grad_hidden[0] * up_pre * second_slope * tangent_pre
    ).astype(jnp.bfloat16)
    partial_sum = jnp.einsum(
        "sxcd,sxcf->xdf", arrived, hess_pre, preferred_element_type=jnp.float32
    )
    summed = lax.psum_scatter(
        partial_sum.astype(jnp.bfloat16), "dp", scatter_dimension=2, tiled=True
    ).astype(jnp.float32)
    loss_scale = 1.0 / math.sqrt(tok_rows * top_count)
    return (summed * loss_scale).astype(jnp.bfloat16)


def plan(mesh):
    shape = dict(mesh.shape)
    fits = shape["groups"] == 1 and shape["expert"] == LINE * 4 and shape["dp"] == 2

    def body(tokens, targets, expert_ids, gate_codes, projections, down_weight, direction):
        everyone = shape["expert"] * shape["dp"] * tokens.size * tokens.dtype.itemsize
        dense = fits and projections.shape[0] == 1 and everyone * 2 <= DENSE_BYTES
        chosen = dense_body if dense else routed_body
        return chosen(
            tokens, targets, expert_ids, gate_codes, projections, down_weight, direction
        )

    return body


def solution(mesh):
    return jax.shard_map(
        plan(mesh),
        mesh=mesh,
        in_specs=(
            P(("groups", "expert", "dp"), None),
            P(("groups", "expert", "dp"), None),
            P(("groups", "expert", "dp"), None),
            P(("groups", "expert", "dp"), None),
            P("expert", None, None, "dp"),
            P("expert", "dp", None),
            P("expert", None, "dp"),
        ),
        out_specs=P(("groups", "expert"), None, "dp"),
        check_vma=False,
    )
```

```python
import functools
import math

import jax
import jax.numpy as jnp
from jax import lax
from jax.experimental import pallas as pl
from jax.experimental.pallas import tpu as pltpu
from jax.sharding import PartitionSpec as P

LINE = 4
VMEM_BYTES = 56 * 1024 * 1024
DENSE_BYTES = 16 * 1024 * 1024


class Place:
    def __init__(self):
        expert = lax.axis_index("expert")
        self.z = expert // 4
        self.y = lax.rem(expert // 2, 2)
        self.c = lax.rem(expert, 2)
        self.x = lax.axis_index("dp")

    def line(self, d):
        return lax.rem(self.z + d, LINE)

    def device(self, z, y, c, x):
        return {"expert": (z * 2 + y) * 2 + c, "dp": x}

    def along_z(self, d):
        return self.device(self.line(d), self.y, self.c, self.x)

    def along_y(self):
        return self.device(self.z, 1 - self.y, self.c, self.x)

    def along_x(self):
        return self.device(self.z, self.y, self.c, 1 - self.x)

    def sibling(self):
        return self.device(self.z, self.y, 1 - self.c, self.x)

    def greet(self):
        barrier = pltpu.get_barrier_semaphore()
        others = [self.along_z(d) for d in range(1, LINE)]
        others += [self.along_y(), self.along_x(), self.sibling()]
        for other in others:
            pl.semaphore_signal(
                barrier, inc=1, device_id=other, device_id_type=pl.DeviceIdType.MESH
            )
        pl.semaphore_wait(barrier, len(others))


def remote(src, dst, send_sem, recv_sem, to):
    return pltpu.make_async_remote_copy(
        src_ref=src,
        dst_ref=dst,
        send_sem=send_sem,
        recv_sem=recv_sem,
        device_id=to,
        device_id_type=pl.DeviceIdType.MESH,
    )


class Spread:
    def __init__(self, me, pieces, send_sem, recv_sem):
        self.me, self.pieces = me, pieces
        self.send_sem, self.recv_sem = send_sem, recv_sem
        self.sends = []
        self.ways = [
            (me.along_y(), me.along_x()) if first == "y" else (me.along_x(), me.along_y())
            for _, first in pieces
        ]

    def copy(self, p, block, to, number):
        ref = self.pieces[p][0](*block)
        return remote(ref, ref, self.send_sem.at[number], self.recv_sem.at[(p,) + block], to)

    def push(self, p, block, to):
        item = self.copy(p, block, to, len(self.sends))
        item.start()
        self.sends.append(item)

    def arrive(self, p, block):
        self.copy(p, block, self.me.sibling(), 0).wait_recv()

    def blocks(self, p, d):
        me, z = self.me, self.me.line(d)
        own = (z, me.y, me.c, me.x)
        by_y = (z, 1 - me.y, me.c, me.x)
        by_x = (z, me.y, me.c, 1 - me.x)
        both = (z, 1 - me.y, me.c, 1 - me.x)
        return (own, by_y, by_x, both) if self.pieces[p][1] == "y" else (own, by_x, by_y, both)

    def start(self):
        for d in range(LINE - 1, 0, -1):
            for p in range(len(self.pieces)):
                self.push(p, self.blocks(p, 0)[0], self.me.along_z(d))

    def line_step(self, d):
        for p in range(len(self.pieces)):
            block = self.blocks(p, d)[0]
            if d:
                self.arrive(p, block)
            self.push(p, block, self.ways[p][0])
            self.push(p, block, self.ways[p][1])
            self.push(p, block, self.me.sibling())

    def first_step(self, d):
        for p in range(len(self.pieces)):
            block = self.blocks(p, d)[1]
            self.arrive(p, block)
            self.push(p, block, self.ways[p][1])
            self.push(p, block, self.me.sibling())

    def second_step(self, d):
        for p in range(len(self.pieces)):
            for block in self.blocks(p, d)[2:]:
                self.arrive(p, block)
                self.push(p, block, self.me.sibling())

    def core_step(self, d):
        for p in range(len(self.pieces)):
            for y in range(2):
                for x in range(2):
                    self.arrive(p, (self.me.line(d), y, 1 - self.me.c, x))

    def finish(self):
        for item in self.sends:
            item.wait_send()


SPREAD_SENDS = 3 + LINE * 5 + LINE * 2


def rows_of(block):
    return block.reshape(-1, block.shape[-1])


def dot(a, b, dims=((1,), (0,))):
    return lax.dot_general(a, b, (dims, ((), ())), preferred_element_type=jnp.float32)


def fused_kernel(
    loss_scale, tok_ref, table_ref, targets, proj_hbm, down_hbm, dir_hbm, hvp_ref,
    all_tok, all_table, proj, down, direction, slope_a, slope_b,
    part, back, total_hvp, core_in, out1, in1, out2, in2, out3, in3,
    weight_sem, core_send, core_recv, send1, recv1, send2, recv2, send3, recv3,
    tok_send, tok_recv, back_send, back_recv,
):
    me = Place()
    expert = lax.axis_index("expert")
    half = tok_ref.shape[1] // 2
    loads = [
        pltpu.make_async_copy(proj_hbm.at[0], proj, weight_sem.at[0]),
        pltpu.make_async_copy(dir_hbm.at[0], direction, weight_sem.at[1]),
        pltpu.make_async_copy(down_hbm.at[0], down, weight_sem.at[2]),
    ]
    for load in loads:
        load.start()
    all_tok[me.z, me.y, me.c, me.x] = tok_ref[...]
    all_table[me.z, me.y, me.c, me.x] = table_ref[...]
    me.greet()
    tok = Spread(
        me,
        [
            (lambda z, y, c, x: all_tok.at[z, y, c, x, :, pl.ds(0, half)], "y"),
            (lambda z, y, c, x: all_tok.at[z, y, c, x, :, pl.ds(half, half)], "x"),
            (lambda z, y, c, x: all_table.at[z, y, c, x], "y"),
        ],
        tok_send,
        tok_recv,
    )
    sends = []

    def push(src, dst, send, recv, to):
        item = remote(src, dst, send, recv, to)
        item.start()
        sends.append(item)
        return item

    def forward(d):
        z = me.line(d)
        rows = rows_of(all_tok[z])
        gate_pre = dot(rows, proj[0])
        up_pre = dot(rows, proj[1])
        tangent_pre = dot(rows, direction[...])
        table = rows_of(all_table[z].astype(jnp.float32))
        named = lax.broadcasted_iota(jnp.int32, table.shape, 1) == expert
        weight = jnp.sum(jnp.where(named, table, 0.0), axis=1, keepdims=True)
        sig = jax.nn.sigmoid(gate_pre)
        rest = 1.0 - sig
        up_weighted = weight * up_pre
        slope = up_weighted * (sig * (1.0 + gate_pre * rest))
        curve = up_weighted * (sig * rest * (2.0 + gate_pre * (1.0 - 2.0 * sig))) * tangent_pre
        slope_a[d] = slope
        slope_b[d] = curve
        hidden = (gate_pre * sig * up_weighted).astype(jnp.bfloat16)
        hidden_tan = (slope * tangent_pre).astype(jnp.bfloat16)
        if d == 0:
            loads[2].wait()
        for k, value in enumerate((hidden, hidden_tan)):
            out = dot(value, down[...]).reshape(part.shape[2:])
            part[k, z] = out.astype(part.dtype)

    core_copies, first, second, third = {}, {}, {}, {}

    def core_send_step(d):
        z = me.line(d)
        core_copies[d] = push(
            part.at[:, z, :, 1 - me.c], core_in.at[:, z], core_send.at[d], core_recv.at[d],
            me.sibling(),
        )

    def pair(h, z, far, near):
        cols = pl.ds(h * half, half)
        y, x = (near, far) if h == 0 else (far, near)
        mine = part[:, z, y, me.c, x, :, cols].astype(jnp.float32)
        return mine + core_in[:, z, y, x, :, cols].astype(jnp.float32)

    axis1 = (me.along_x(), me.along_y())
    axis2 = (me.along_y(), me.along_x())
    far_own = (me.x, me.y)
    near_own = (me.y, me.x)

    def sum_first(d):
        core_copies[d].wait_recv()
        for h in range(2):
            for near in range(2):
                out1[h, d, near] = pair(h, me.line(d), 1 - far_own[h], near).astype(out1.dtype)
            first[d, h] = push(
                out1.at[h, d], in1.at[h, d], send1.at[h, d], recv1.at[h, d], axis1[h]
            )

    def sum_second(d):
        for h in range(2):
            first[d, h].wait_recv()
            near = 1 - near_own[h]
            total = pair(h, me.line(d), far_own[h], near) + in1[h, d, near].astype(jnp.float32)
            out2[h, d] = total.astype(out2.dtype)
            second[d, h] = push(
                out2.at[h, d], in2.at[h, d], send2.at[h, d], recv2.at[h, d], axis2[h]
            )

    def plane_total(d, h):
        second[d, h].wait_recv()
        near = near_own[h]
        total = pair(h, me.line(d), far_own[h], near) + in1[h, d, near].astype(jnp.float32)
        return total + in2[h, d].astype(jnp.float32)

    def sum_third(d):
        for h in range(2):
            out3[h, d - 1] = plane_total(d, h).astype(out3.dtype)
            third[d, h] = push(
                out3.at[h, d - 1], in3.at[h, d - 1], send3.at[h, d - 1], recv3.at[h, d - 1],
                me.along_z(d),
            )

    tok.start()
    tok.line_step(0)
    tok.first_step(0)
    tok.line_step(1)
    tok.second_step(0)
    tok.first_step(1)
    tok.core_step(0)
    loads[0].wait()
    loads[1].wait()
    forward(0)
    core_send_step(0)
    tok.line_step(2)
    tok.second_step(1)
    tok.first_step(2)
    tok.core_step(1)
    forward(1)
    core_send_step(1)
    tok.line_step(3)
    tok.second_step(2)
    tok.first_step(3)
    tok.core_step(2)
    sum_first(1)
    forward(2)
    core_send_step(2)
    tok.second_step(3)
    tok.core_step(3)
    sum_first(2)
    sum_second(1)
    forward(3)
    core_send_step(3)
    sum_first(3)
    sum_third(1)
    sum_second(2)
    sum_third(2)
    sum_first(0)
    sum_second(3)
    sum_third(3)
    sum_second(0)

    spread = Spread(
        me,
        [
            (lambda z, y, c, x: back.at[:, z, y, c, x, :, pl.ds(0, half)], "y"),
            (lambda z, y, c, x: back.at[:, z, y, c, x, :, pl.ds(half, half)], "x"),
        ],
        back_send,
        back_recv,
    )
    for h in range(2):
        cols = pl.ds(h * half, half)
        total = plane_total(0, h)
        for d in range(1, LINE):
            third[d, h].wait_recv()
            total = total + in3[h, d - 1].astype(jnp.float32)
        residual = total[0] - targets[:, cols].astype(jnp.float32)
        back[0, me.z, me.y, me.c, me.x, :, cols] = residual.astype(back.dtype)
        back[1, me.z, me.y, me.c, me.x, :, cols] = total[1].astype(back.dtype)

    def backward(d):
        z = me.line(d)
        grad_hidden = dot(rows_of(back[0, z]), down[...], ((1,), (1,)))
        grad_tangent = dot(rows_of(back[1, z]), down[...], ((1,), (1,)))
        hess_pre = (grad_tangent * slope_a[d] + grad_hidden * slope_b[d]).astype(jnp.bfloat16)
        term = dot(rows_of(all_tok[z]), hess_pre, ((0,), (0,)))
        if d == 0:
            total_hvp[...] = term
        elif d < LINE - 1:
            total_hvp[...] += term
        else:
            hvp_ref[0] = ((total_hvp[...] + term) * loss_scale).astype(hvp_ref.dtype)

    spread.start()
    spread.line_step(0)
    spread.first_step(0)
    spread.line_step(1)
    spread.second_step(0)
    spread.first_step(1)
    spread.core_step(0)
    spread.line_step(2)
    backward(0)
    spread.second_step(1)
    spread.first_step(2)
    spread.core_step(1)
    spread.line_step(3)
    backward(1)
    spread.first_step(3)
    spread.second_step(2)
    spread.core_step(2)
    backward(2)
    spread.second_step(3)
    spread.core_step(3)
    backward(3)
    tok.finish()
    spread.finish()
    for item in sends:
        item.wait_send()


def dense_body(tokens, targets, expert_ids, gate_codes, projections, down_weight, direction):
    rows, width = tokens.shape
    units = down_weight.shape[1]
    top_count = expert_ids.shape[1]
    half = width // 2
    grid = (LINE, 2, 2, 2)
    plane_rows = 8 * rows
    kind = tokens.dtype
    lanes = jnp.arange(128, dtype=jnp.int32)
    named = expert_ids.T[:, :, None] == lanes[None, None, :]
    table = jnp.sum(jnp.where(named, gate_codes.T[:, :, None], 0), axis=0)
    table = (table.astype(jnp.float32) / 256.0).astype(jnp.bfloat16)
    vmem = pl.BlockSpec(memory_space=pltpu.VMEM)
    hbm = pl.BlockSpec(memory_space=pl.ANY)
    dma = pltpu.SemaphoreType.DMA
    return pl.pallas_call(
        functools.partial(fused_kernel, 1.0 / math.sqrt(rows * top_count)),
        out_shape=jax.ShapeDtypeStruct((1, width, units), jnp.bfloat16),
        in_specs=[vmem] * 3 + [hbm] * 3,
        out_specs=vmem,
        scratch_shapes=[
            pltpu.VMEM(grid + (rows, width), kind),
            pltpu.VMEM(grid + (rows, 128), kind),
            pltpu.VMEM((2, width, units), kind),
            pltpu.VMEM((units, width), kind),
            pltpu.VMEM((width, units), kind),
            pltpu.VMEM((LINE, plane_rows, units), jnp.float32),
            pltpu.VMEM((LINE, plane_rows, units), jnp.float32),
            pltpu.VMEM((2,) + grid + (rows, width), kind),
            pltpu.VMEM((2,) + grid + (rows, width), kind),
            pltpu.VMEM((width, units), jnp.float32),
            pltpu.VMEM((2, LINE, 2, 2, rows, width), kind),
            pltpu.VMEM((2, LINE, 2, 2, rows, half), kind),
            pltpu.VMEM((2, LINE, 2, 2, rows, half), kind),
            pltpu.VMEM((2, LINE, 2, rows, half), kind),
            pltpu.VMEM((2, LINE, 2, rows, half), kind),
            pltpu.VMEM((2, LINE - 1, 2, rows, half), kind),
            pltpu.VMEM((2, LINE - 1, 2, rows, half), kind),
            dma((3,)),
            dma((LINE,)),
            dma((LINE,)),
            dma((2, LINE)),
            dma((2, LINE)),
            dma((2, LINE)),
            dma((2, LINE)),
            dma((2, LINE - 1)),
            dma((2, LINE - 1)),
            dma((3 * SPREAD_SENDS,)),
            dma((3,) + grid),
            dma((2 * SPREAD_SENDS,)),
            dma((2,) + grid),
        ],
        compiler_params=pltpu.CompilerParams(
            collective_id=0, has_side_effects=True, vmem_limit_bytes=VMEM_BYTES
        ),
    )(tokens, table, targets, projections, down_weight, direction)


def slot_tables(route_ids, expert_total, slot_cap):
    routed_flat = route_ids.reshape(-1)
    route_count = routed_flat.shape[0]
    onehot = (routed_flat[:, None] == jnp.arange(expert_total, dtype=jnp.int32)[None, :]).astype(
        jnp.int32
    )
    earlier = jnp.cumsum(onehot, axis=0) - onehot
    within_slot = jnp.sum(earlier * onehot, axis=1)
    landing = routed_flat * slot_cap + within_slot
    source_route = (
        jnp.zeros((expert_total * slot_cap,), jnp.int32)
        .at[landing]
        .set(jnp.arange(route_count, dtype=jnp.int32))
    )
    occupied = jnp.zeros((expert_total * slot_cap,), jnp.int32).at[landing].set(1)
    return (landing, source_route, occupied)


def routed_body(tokens, targets, expert_ids, gate_codes, projections, down_weight, direction):
    tok_rows, model_width = tokens.shape
    top_count = expert_ids.shape[1]
    local_experts = projections.shape[0]
    expert_devs = lax.axis_size("expert")
    all_experts = local_experts * expert_devs
    slot_cap = max(2, tok_rows * top_count // all_experts + 1)
    landing, source_route, occupied = slot_tables(expert_ids, all_experts, slot_cap)
    source_token = source_route // top_count
    send_rows = jnp.where(occupied[:, None] > 0, tokens[source_token], jnp.zeros((), tokens.dtype))
    send_rows = send_rows.reshape(expert_devs, local_experts, slot_cap, model_width)
    arrived = lax.all_to_all(send_rows, "expert", split_axis=0, concat_axis=0, tiled=True)
    pair_pre = jnp.einsum(
        "sxcd,xkdf->ksxcf",
        arrived,
        lax.all_gather(projections, "dp", axis=3, tiled=True),
        preferred_element_type=jnp.float32,
    )
    tangent_pre = jnp.einsum(
        "sxcd,xdf->sxcf",
        arrived,
        lax.all_gather(direction, "dp", axis=2, tiled=True),
        preferred_element_type=jnp.float32,
    )
    gate_pre = pair_pre[0]
    up_pre = pair_pre[1]
    down_full = lax.all_gather(down_weight, "dp", axis=1, tiled=True)
    sigmoid_val = jax.nn.sigmoid(gate_pre)
    first_slope = sigmoid_val * (1.0 + gate_pre * (1.0 - sigmoid_val))
    second_slope = sigmoid_val * (1.0 - sigmoid_val) * (2.0 + gate_pre * (1.0 - 2.0 * sigmoid_val))
    hidden = (gate_pre * sigmoid_val * up_pre).astype(jnp.bfloat16)
    hidden_tan = (first_slope * tangent_pre * up_pre).astype(jnp.bfloat16)
    stacked_hidden = jnp.stack([hidden, hidden_tan])
    expert_out = jnp.einsum(
        "ksxcf,xfd->ksxcd", stacked_hidden, down_full, preferred_element_type=jnp.float32
    ).astype(jnp.bfloat16)
    returned = lax.all_to_all(expert_out, "expert", split_axis=1, concat_axis=1, tiled=True)
    slot_out = returned.reshape(2, all_experts * slot_cap, model_width)
    route_out = slot_out[:, landing].astype(jnp.float32)
    route_weight = gate_codes.reshape(-1).astype(jnp.float32) / 256.0
    combined = jnp.sum(
        (route_out * route_weight[None, :, None]).reshape(2, tok_rows, top_count, model_width),
        axis=2,
    )
    residual = combined[0] - targets.astype(jnp.float32)
    pair_res = jnp.stack([residual, combined[1]])
    slot_weight = jnp.where(occupied > 0, route_weight[source_route], jnp.zeros((), jnp.float32))
    outgoing = (pair_res[:, source_token] * slot_weight[None, :, None]).astype(jnp.bfloat16)
    outgoing = outgoing.reshape(2, expert_devs, local_experts, slot_cap, model_width)
    incoming = lax.all_to_all(outgoing, "expert", split_axis=1, concat_axis=1, tiled=True)
    grad_hidden = jnp.einsum(
        "ksxcd,xfd->ksxcf", incoming, down_full, preferred_element_type=jnp.float32
    )
    hess_pre = (
        grad_hidden[1] * up_pre * first_slope + grad_hidden[0] * up_pre * second_slope * tangent_pre
    ).astype(jnp.bfloat16)
    partial_sum = jnp.einsum(
        "sxcd,sxcf->xdf", arrived, hess_pre, preferred_element_type=jnp.float32
    )
    summed = lax.psum_scatter(
        partial_sum.astype(jnp.bfloat16), "dp", scatter_dimension=2, tiled=True
    ).astype(jnp.float32)
    loss_scale = 1.0 / math.sqrt(tok_rows * top_count)
    return (summed * loss_scale).astype(jnp.bfloat16)


def plan(mesh):
    shape = dict(mesh.shape)
    fits = shape["groups"] == 1 and shape["expert"] == LINE * 4 and shape["dp"] == 2

    def body(tokens, targets, expert_ids, gate_codes, projections, down_weight, direction):
        everyone = shape["expert"] * shape["dp"] * tokens.size * tokens.dtype.itemsize
        dense = fits and projections.shape[0] == 1 and everyone * 2 <= DENSE_BYTES
        chosen = dense_body if dense else routed_body
        return chosen(
            tokens, targets, expert_ids, gate_codes, projections, down_weight, direction
        )

    return body


def solution(mesh):
    return jax.shard_map(
        plan(mesh),
        mesh=mesh,
        in_specs=(
            P(("groups", "expert", "dp"), None),
            P(("groups", "expert", "dp"), None),
            P(("groups", "expert", "dp"), None),
            P(("groups", "expert", "dp"), None),
            P("expert", None, None, "dp"),
            P("expert", "dp", None),
            P("expert", None, "dp"),
        ),
        out_specs=P(("groups", "expert"), None, "dp"),
        check_vma=False,
    )
```
